256 devices in a mesh: mod: 8 (over x_lo, y), blk: 32 (over z, x_hi, core).
Axes of the slice: x: 4 (x_hi: 2, x_lo: 2; x = x_hi * 2 + x_lo), y: 4, z: 8, core: 2. Of those that a mesh axis runs over, the one named last changes fastest.
Arguments:
- train_grads: float32 [8, 20480, 4096], P('mod', 'blk'), may hold values from -6 to 6
- left_factor: float32 [8, 64, 64], P('mod'), may hold values from -0.75 to 0.75
- right_factor: float32 [8, 64, 64], P('mod'), may hold values from -0.75 to 0.75
- queries: float32 [8, 1024, 4096], P('mod', 'blk'), may hold values from -0.03125 to 0.03125
- owners: int32 [32], replicated, may hold values from 0 to 31, each once
- range_start: int32 [32], replicated, may hold values from 0 to 10240
Outputs:
- scores: float32 [1024, 20480], P('mod', 'blk')
The draws below stay inside these ranges and needn't reach their ends.
Inputs may be any that keep to these rules, and one draw needn't show every extreme that they name: owners is a permutation of the 32 block numbers.
All inputs are finite; a program needn't handle non-finite values.
Results may differ from the reference program's by a relative error of at most 0.0001.
Values sent between devices are 32-bit elements; how exact they have to be, the bound alone decides.
No kernel may reach another device: no remote copies, remote signals or barrier semaphores. Data moves between devices by JAX's collectives and lax.ppermute only.
A program may use at most 128 MiB of HBM per device.

```python
import jax
import jax.numpy as jnp
from jax import lax

K = 64
FEAT = 4096
QB = 32
MODS = 8
BLOCKS = 32
NTRAIN = 20480
NQ = 1024
WINDOW = 10240


def place_ends(drawn, rng, smallest, top_value):
    longest = drawn.shape.index(max(drawn.shape))
    spots = []
    for shift in (0, 1):
        where = [jax.random.randint(jax.random.fold_in(rng, axis), (), 0, length) for axis, length in enumerate(drawn.shape)]
        where[longest] = (where[longest] + shift) % drawn.shape[longest]
        spots.append(tuple(where))
    return drawn.at[spots[0]].set(smallest).at[spots[1]].set(top_value)


def steps_of(rng, shape, cuts, low, largest):
    factor_of, own = 1.0, jax.random.fold_in(rng, 6)
    for dim, parts in cuts:
        steps = jnp.exp(jax.random.uniform(jax.random.fold_in(own, dim), (parts,), jnp.float32, low / len(cuts), largest / len(cuts)))
        factor_of = factor_of * jnp.repeat(steps, shape[dim] // parts).reshape([-1 if axis == dim else 1 for axis in range(len(shape))])
    return factor_of


def noise(own_key, dims, width, limit, pieces=(), held_as=jnp.bfloat16):
    level = steps_of(own_key, dims, pieces, -0.22, 0.18) if pieces else 1.0
    values = jax.random.normal(own_key, dims, jnp.float32) * width * level
    return jnp.minimum(jnp.maximum(values, -limit), limit).astype(held_as)


def setup_inputs(seed: int = 0) -> dict:
    key_list = jax.random.split(jax.random.key(seed), 7)
    train_grads = noise(key_list[0], (MODS, NTRAIN, FEAT), 1.0, 6.0, ((0, 8), (1, 32)), jnp.float32)
    left_factor = noise(key_list[1], (MODS, K, K), K ** -0.5, 0.75, ((0, 8),), jnp.float32)
    right_factor = noise(key_list[2], (MODS, K, K), K ** -0.5, 0.75, ((0, 8),), jnp.float32)
    queries = noise(key_list[3], (MODS, NQ, FEAT), (FEAT * MODS) ** -0.5, 0.03125, ((0, 8), (1, 32)), jnp.float32)
    owners = jax.random.permutation(key_list[4], BLOCKS).astype(jnp.int32)
    range_start = place_ends(jax.random.randint(key_list[5], (BLOCKS,), 0, NTRAIN - WINDOW + 1), jax.random.fold_in(key_list[5], 1), 0, NTRAIN - WINDOW).astype(jnp.int32)
    return {"train_grads": train_grads, "left_factor": left_factor, "right_factor": right_factor, "queries": queries, "owners": owners, "range_start": range_start}


def reference(train_grads, left_factor, right_factor, queries, owners, range_start):
    highest = lax.Precision.HIGHEST

    def module_step(carry, operands):
        grads, lfac, rfac, query = operands
        rows = grads.reshape(NTRAIN, K, K)
        middle = jnp.einsum('ba,rbc->rac', lfac, rows, precision=highest)
        refreshed = jnp.einsum('rac,cd->rad', middle, rfac, precision=highest).reshape(NTRAIN, FEAT)
        part = jnp.dot(query, refreshed.T, precision=highest, preferred_element_type=jnp.float32)
        return (carry + part, None)
    start = jnp.zeros((NQ, NTRAIN), jnp.float32)
    total, _ = lax.scan(module_step, start, (train_grads, left_factor, right_factor, queries))
    squares = lax.optimization_barrier(jnp.sum(train_grads * train_grads, axis=(0, 2)))
    row_scale = lax.rsqrt(squares / (MODS * FEAT) + 1e-06)
    qrow = jnp.arange(NQ, dtype=jnp.int32)
    dest = owners[qrow // QB] * QB + qrow % QB
    permuted = jnp.zeros((NQ, NTRAIN), jnp.float32).at[dest].set(total)
    starts = range_start[qrow // QB]
    cols = jnp.arange(NTRAIN, dtype=jnp.int32)
    inside = (cols[None, :] >= starts[:, None]) & (cols[None, :] < starts[:, None] + WINDOW)
    return jnp.where(inside, permuted * row_scale[None, :], jnp.float32(0.0))
```

```python
import functools

import jax
import jax.numpy as jnp
from jax import lax
from jax.experimental import pallas as pl
from jax.experimental.pallas import tpu as pltpu
from jax.sharding import PartitionSpec as P

NZ = 8
NY = 4
FEAT_STEP = 512


def blk_pairs(move):
    return [
        (z * 4 + h * 2 + c, move(z, h, c))
        for z in range(NZ)
        for h in range(2)
        for c in range(2)
    ]


Z_UP = blk_pairs(lambda z, h, c: (z + 1) % NZ * 4 + h * 2 + c)
Z_DOWN = blk_pairs(lambda z, h, c: (z - 1) % NZ * 4 + h * 2 + c)
X_FAR = blk_pairs(lambda z, h, c: z * 4 + (1 - h) * 2 + c)
CORE = blk_pairs(lambda z, h, c: z * 4 + h * 2 + 1 - c)
Y_BY = [[(x * 4 + y, x * 4 + (y + k) % NY) for x in range(2) for y in range(NY)] for k in range(NY)]
X_NEAR = [(x * 4 + y, (1 - x) * 4 + y) for x in range(2) for y in range(NY)]


def up(block):
    return lax.ppermute(block, "blk", Z_UP)


def down(block):
    return lax.ppermute(block, "blk", Z_DOWN)


def far(block):
    return lax.ppermute(block, "blk", X_FAR)


def other(block):
    return lax.ppermute(block, "blk", CORE)


def split(value):
    high = value.astype(jnp.bfloat16)
    low = (value - high.astype(jnp.float32)).astype(jnp.bfloat16)
    return high, low


def nt(a, b):
    return lax.dot_general(a, b, (((1,), (1,)), ((), ())), preferred_element_type=jnp.float32)


def score_kernel(npieces, squares, y_ref, g_ref, *refs):
    pieces = refs[:npieces]
    outs = refs[npieces : npieces + NY]
    acc = refs[npieces + NY]
    sq = refs[npieces + NY + 1] if squares else None
    step = pl.program_id(0)
    g = g_ref[...]
    ghi, glo = split(g)
    q = jnp.concatenate([p[...] for p in pieces], axis=0)
    qhi, qlo = split(q)
    part = nt(ghi, qhi) + (nt(ghi, qlo) + nt(glo, qhi))

    @pl.when(step == 0)
    def _():
        acc[...] = part

    @pl.when(step > 0)
    def _():
        acc[...] += part

    if squares:
        sums = jnp.broadcast_to(jnp.sum(g * g, axis=1, keepdims=True), sq.shape)

        @pl.when(step == 0)
        def _():
            sq[...] = sums

        @pl.when(step > 0)
        def _():
            sq[...] += sums

    @pl.when(step == pl.num_programs(0) - 1)
    def _():
        y = y_ref[0]
        rows = acc.shape[0] // NY
        for k in range(NY):
            first = pl.multiple_of(((y + k) % NY) * rows, 8)
            outs[k][0:rows, :] = acc[pl.ds(first, rows), :]
            if squares:
                outs[k][rows:, :] = jnp.zeros((8, outs[k].shape[1]), jnp.float32)
                outs[k][rows:, 0:rows] = jnp.transpose(sq[pl.ds(first, rows), 0:8])


def scores_of(y, grads, pieces, squares):
    rows, feat = grads.shape
    width = sum(p.shape[0] for p in pieces)
    slice_rows = rows // NY + (8 if squares else 0)
    scratch = [pltpu.VMEM((rows, width), jnp.float32)]
    if squares:
        scratch.append(pltpu.VMEM((rows, 128), jnp.float32))
    return pl.pallas_call(
        functools.partial(score_kernel, len(pieces), squares),
        grid_spec=pltpu.PrefetchScalarGridSpec(
            num_scalar_prefetch=1,
            grid=(feat // FEAT_STEP,),
            in_specs=[pl.BlockSpec((rows, FEAT_STEP), lambda i, y: (0, i))]
            + [pl.BlockSpec((p.shape[0], FEAT_STEP), lambda i, y: (0, i)) for p in pieces],
            out_specs=[pl.BlockSpec((slice_rows, width), lambda i, y: (0, 0))] * NY,
            scratch_shapes=scratch,
        ),
        out_shape=[jax.ShapeDtypeStruct((slice_rows, width), jnp.float32)] * NY,
        compiler_params=pltpu.CompilerParams(vmem_limit_bytes=40 * 1024 * 1024),
    )(y, grads, *pieces)


def reduce_slices(slices, xl):
    rows = slices[0].shape[0] // 16 * 16 // 2
    got = [lax.ppermute(slices[k], "mod", Y_BY[k]) for k in range(1, NY)]
    total = slices[0] + got[0] + (got[1] + got[2])
    half = 80
    keep = lax.dynamic_slice_in_dim(total, xl * half, half, 0)
    send = lax.dynamic_slice_in_dim(total, (1 - xl) * half, half, 0)
    extra = total[2 * half :]
    if extra.shape[0]:
        send = jnp.concatenate([send, extra], axis=0)
    back = lax.ppermute(send, "mod", X_NEAR)
    if extra.shape[0]:
        return keep + back[:half], extra[0] + back[half]
    return keep + back


def shards(train_grads, left_factor, right_factor, queries, owners, range_start):
    highest = lax.Precision.HIGHEST
    nmods = lax.axis_size("mod")
    nblk = lax.axis_size("blk")
    rows_dev = train_grads.shape[1]
    feat = train_grads.shape[2]
    side = left_factor.shape[1]
    qblock = queries.shape[1]
    half = qblock // 2
    window = rows_dev * nblk // 2
    share = rows_dev // nmods
    grads = train_grads[0]
    m = lax.axis_index("mod")
    b = lax.axis_index("blk")
    xl, y = m // NY, m % NY
    z, h, c = b // 4, (b // 2) % 2, b % 2
    yarr = jnp.reshape(y, (1,)).astype(jnp.int32)

    mats = queries[0].reshape(qblock, side, side)
    mats = jnp.einsum("rad,cd->rac", mats, right_factor[0], precision=highest)
    mats = jnp.einsum("ba,rac->rbc", left_factor[0], mats, precision=highest)
    own = mats.reshape(qblock, feat)

    A, E = {0: own}, {}
    A[-1], A[1], E[0] = up(A[0]), down(A[0]), far(A[0])
    A[-2], A[2], E[1] = up(A[-1]), down(A[1]), far(A[1])
    A[-3], A[3], E[-1] = up(A[-2]), down(A[2]), far(A[-1])
    lo = lambda v: v[:half]
    hi = lambda v: v[half:]
    A4 = [up(lo(A[-3])), down(hi(A[3]))]
    E2m = [up(lo(E[-1])), None]
    E2p = [down(lo(E[1])), None]
    E3p, E3m = [None, far(hi(A[3]))], [None, far(hi(A[-3]))]
    E2m[1] = up(hi(E[-1]))
    E2p[1] = down(hi(E[1]))
    E3m[0] = up(E2m[0])
    E3p[0] = down(E2p[0])
    E4 = [far(A4[0]), far(A4[1])]

    chunks = [
        [(A[0], 0, 0, 0, 2), (A[-1], -1, 0, 0, 2), (A[1], 1, 0, 0, 2), (E[0], 0, 1, 0, 2)],
        [(A[-2], -2, 0, 0, 2), (A[2], 2, 0, 0, 2), (E[1], 1, 1, 0, 2), (E[-1], -1, 1, 0, 2)],
        [(A[-3], -3, 0, 0, 2), (A[3], 3, 0, 0, 2), (A4[0], 4, 0, 0, 1), (A4[1], 4, 0, 1, 1),
         (E2m[0], -2, 1, 0, 1), (E2p[0], 2, 1, 0, 1)],
        [(E3m[1], -3, 1, 1, 1), (E3p[1], 3, 1, 1, 1), (E2m[1], -2, 1, 1, 1), (E2p[1], 2, 1, 1, 1),
         (E3m[0], -3, 1, 0, 1), (E3p[0], 3, 1, 0, 1), (E4[0], 4, 1, 0, 1), (E4[1], 4, 1, 1, 1)],
    ]
    halves, totals, squares = [], [], None
    for index, chunk in enumerate(chunks):
        pieces = [p[0] for p in chunk] + [other(p[0]) for p in chunk]
        for flip in range(2):
            for _, d, col, first, count in chunk:
                block = (z + d) % NZ * 4 + (h + col) % 2 * 2 + (c + flip) % 2
                halves += [block * 2 + first + k for k in range(count)]
        slices = scores_of(yarr, grads, pieces, index == 0)
        if index == 0:
            total, squares = reduce_slices(slices, xl)
        else:
            total = reduce_slices(slices, xl)
        totals.append(total)

    source = jnp.stack(halves).astype(jnp.int32)
    blocks = jnp.arange(nblk, dtype=jnp.int32)
    target = jnp.sum(jnp.where((source // 2)[:, None] == blocks[None, :], owners[None, :], 0), axis=1)
    dest = ((target * 2 + source % 2) * half)[:, None] + jnp.arange(half, dtype=jnp.int32)[None, :]
    dest = dest.reshape(-1)
    nq = dest.shape[0]
    pick = (jnp.arange(nq, dtype=jnp.int32)[:, None] == dest[None, :]).astype(jnp.float32)
    stacked = jnp.concatenate(totals, axis=1)
    placed = lax.dot_general(pick, stacked, (((1,), (1,)), ((), ())), precision=highest,
                             preferred_element_type=jnp.float32)
    mine = lax.dynamic_slice_in_dim(squares, xl * share, share, 0)
    row_scale = lax.rsqrt(mine / (nmods * feat) + 1e-06)
    placed = placed * row_scale[None, :]
    got = lax.all_to_all(placed.reshape(nmods, nq // nmods, share), "mod", 0, 0)
    got = got.reshape(2, NY, nq // nmods, share).transpose(2, 1, 0, 3).reshape(nq // nmods, rows_dev)
    row_ids = b * rows_dev + jnp.arange(rows_dev, dtype=jnp.int32)
    out_block = m * (nblk // nmods) + jnp.arange(nq // nmods, dtype=jnp.int32) // qblock
    first = jnp.sum(jnp.where(out_block[:, None] == blocks[None, :], range_start[None, :], 0), axis=1)
    inside = (row_ids[None, :] >= first[:, None]) & (row_ids[None, :] < first[:, None] + window)
    return jnp.where(inside, got, jnp.float32(0.0))


def solution(mesh):
    in_specs = (
        P("mod", "blk", None),
        P("mod", None, None),
        P("mod", None, None),
        P("mod", "blk", None),
        P(),
        P(),
    )
    out_specs = P("mod", "blk")
    return jax.shard_map(shards, mesh=mesh, in_specs=in_specs, out_specs=out_specs, check_vma=False)
```

```python
import functools

import jax
import jax.numpy as jnp
from jax import lax
from jax.experimental import pallas as pl
from jax.experimental.pallas import tpu as pltpu
from jax.sharding import PartitionSpec as P

NZ = 8
NY = 4
FEAT_STEP = 1024
VMEM_LIMIT = 16 * 1024 * 1024


def blk_pairs(move):
    return [
        (z * 4 + h * 2 + c, move(z, h, c))
        for z in range(NZ)
        for h in range(2)
        for c in range(2)
    ]


Z_UP = blk_pairs(lambda z, h, c: (z + 1) % NZ * 4 + h * 2 + c)
Z_DOWN = blk_pairs(lambda z, h, c: (z - 1) % NZ * 4 + h * 2 + c)
X_FAR = blk_pairs(lambda z, h, c: z * 4 + (1 - h) * 2 + c)
CORE = blk_pairs(lambda z, h, c: z * 4 + h * 2 + 1 - c)
Y_GROUPS = [[x * 4 + y for y in range(NY)] for x in range(2)]


def up(block):
    return lax.ppermute(block, "blk", Z_UP)


def down(block):
    return lax.ppermute(block, "blk", Z_DOWN)


def far(block):
    return lax.ppermute(block, "blk", X_FAR)


def other(block):
    return lax.ppermute(block, "blk", CORE)


def split(value):
    high = value.astype(jnp.bfloat16)
    low = (value - high.astype(jnp.float32)).astype(jnp.bfloat16)
    return high, low


def nt(a, b):
    return lax.dot_general(a, b, (((1,), (1,)), ((), ())), preferred_element_type=jnp.float32)


def split_kernel(g_ref, hi_ref, lo_ref, sq_ref):
    rows = g_ref.shape[0]
    here = pl.ds(pl.multiple_of(pl.program_id(0) * rows, rows), rows)
    g = g_ref[...]
    hi_ref[here, :], lo_ref[here, :] = split(g)
    sq_ref[here, :] = jnp.broadcast_to(jnp.sum(g * g, axis=1, keepdims=True), (rows, 128))


def split_grads(grads):
    rows, feat = grads.shape
    whole = pl.BlockSpec(memory_space=pltpu.VMEM)
    return pl.pallas_call(
        split_kernel,
        grid=(rows // 128,),
        in_specs=[pl.BlockSpec((128, feat), lambda i: (i, 0))],
        out_specs=[whole, whole, whole],
        out_shape=[
            pltpu.VMEM((rows, feat), jnp.bfloat16),
            pltpu.VMEM((rows, feat), jnp.bfloat16),
            pltpu.VMEM((rows, 128), jnp.float32),
        ],
        compiler_params=pltpu.CompilerParams(vmem_limit_bytes=VMEM_LIMIT),
    )(pltpu.with_memory_space_constraint(grads, pltpu.HBM))


def score_kernel(spans, squares, hi_ref, lo_ref, *refs):
    if squares:
        sq_ref, *refs = refs
    pieces = refs[: len(spans)]
    out_ref, acc = refs[len(spans) :]
    rows, feat = hi_ref.shape
    for start in range(0, feat, FEAT_STEP):
        part = slice(start, start + FEAT_STEP)
        q = jnp.concatenate([p[a:b, part] for p, (a, b) in zip(pieces, spans)], axis=0)
        qhi, qlo = split(q)
        ghi, glo = hi_ref[:, part], lo_ref[:, part]
        value = nt(ghi, qhi) + (nt(ghi, qlo) + nt(glo, qhi))
        if start == 0:
            acc[...] = value
        else:
            acc[...] += value
    count = rows // NY
    for k in range(NY):
        here = slice(k * count, (k + 1) * count)
        out_ref[k, 0:count, :] = acc[here, :]
        if squares:
            out_ref[k, count:, :] = jnp.zeros((8, out_ref.shape[2]), jnp.float32)
            out_ref[k, count:, 0:count] = jnp.transpose(sq_ref[here, 0:8])


def scores_of(grads, pieces, squares=None):
    hi, lo = (pltpu.with_memory_space_constraint(g, pltpu.VMEM) for g in grads)
    rows = hi.shape[0]
    spans = [(first, first + count) for _, first, count in pieces]
    width = sum(count for _, _, count in pieces)
    slice_rows = rows // NY + (0 if squares is None else 8)
    whole = pl.BlockSpec(memory_space=pltpu.VMEM)
    extra = [] if squares is None else [squares]
    flops = 6 * rows * width * hi.shape[1]
    return pl.pallas_call(
        functools.partial(score_kernel, spans, squares is not None),
        in_specs=[whole] * (2 + len(extra) + len(pieces)),
        out_specs=whole,
        out_shape=jax.ShapeDtypeStruct((NY, slice_rows, width), jnp.float32),
        scratch_shapes=[pltpu.VMEM((rows, width), jnp.float32)],
        compiler_params=pltpu.CompilerParams(vmem_limit_bytes=VMEM_LIMIT),
        cost_estimate=pl.CostEstimate(flops=flops, bytes_accessed=4 * 1024 * 1024, transcendentals=0),
    )(hi, lo, *extra, *[p[0] for p in pieces])


def over_y(slices):
    return lax.all_to_all(slices, "mod", 0, 0, axis_index_groups=Y_GROUPS)


def pack_kernel(plans, *refs):
    blocks, outs = refs[: -len(plans)], refs[-len(plans) :]
    for out, plan in zip(outs, plans):
        at = 0
        for which, first, count in plan:
            out[at : at + count, :] = blocks[which][first : first + count, :]
            at += count


def pack(blocks, *plans):
    whole = pl.BlockSpec(memory_space=pltpu.VMEM)
    return pl.pallas_call(
        functools.partial(pack_kernel, plans),
        in_specs=[whole] * len(blocks),
        out_specs=[whole] * len(plans),
        out_shape=[
            jax.ShapeDtypeStruct((sum(p[2] for p in plan), blocks[0].shape[1]), jnp.float32)
            for plan in plans
        ],
        compiler_params=pltpu.CompilerParams(vmem_limit_bytes=VMEM_LIMIT),
    )(*blocks)


def place_kernel(dest_ref, *refs):
    *parts, out_ref = refs
    sums = [p[0] + p[1] + (p[2] + p[3]) for p in parts]
    count = parts[-1].shape[1]
    total = jnp.concatenate([v[:count] for v in sums], axis=1)
    high = total.astype(jnp.bfloat16)
    rest = total - high.astype(jnp.float32)
    mid = rest.astype(jnp.bfloat16)
    low = (rest - mid.astype(jnp.float32)).astype(jnp.bfloat16)
    stacked = jnp.concatenate([high, mid, low], axis=0)
    squares = sums[0][count:, :]
    row = lax.broadcasted_iota(jnp.int32, (8, 128), 0)
    tail = jnp.where(row == 0, squares[:, 0:128], squares[:, 128:256])
    nq = dest_ref.shape[0]
    lane = lax.broadcasted_iota(jnp.int32, (nq, 256), 1)
    for first in range(0, nq, 256):
        pick = jnp.where(dest_ref[...] == lane + first, 1.0, 0.0).astype(jnp.bfloat16)
        moved = jnp.dot(stacked, pick, preferred_element_type=jnp.float32)
        moved = moved[:count] + (moved[count : 2 * count] + moved[2 * count :])
        for k in range(2):
            out_ref[first // 128 + k, 0:count, :] = moved[:, k * 128 : (k + 1) * 128]
            out_ref[first // 128 + k, count:, :] = tail


def place(dest, parts):
    whole = pl.BlockSpec(memory_space=pltpu.VMEM)
    nq = dest.shape[0]
    return pl.pallas_call(
        place_kernel,
        in_specs=[whole] * (1 + len(parts)),
        out_specs=whole,
        out_shape=jax.ShapeDtypeStruct((nq // 128, parts[0].shape[1], 128), jnp.float32),
        compiler_params=pltpu.CompilerParams(vmem_limit_bytes=VMEM_LIMIT),
    )(dest[:, None], *parts)


def finish_kernel(window, terms, base_ref, first_ref, got_ref, out_ref):
    rows = got_ref.shape[1] - 8
    both = [got_ref[k] + got_ref[NY + k] for k in range(NY)]
    values = jnp.transpose(jnp.concatenate([v[:rows] for v in both], axis=0))
    squares = jnp.concatenate(
        [w for v in both for w in (v[rows : rows + 1, :], v[rows + 1 : rows + 2, : rows - 128])],
        axis=1,
    )
    scale = lax.rsqrt(squares / terms + 1e-06)
    ids = base_ref[0] + lax.broadcasted_iota(jnp.int32, values.shape, 1)
    first = first_ref[...]
    inside = (ids >= first) & (ids < first + window)
    out_ref[...] = jnp.where(inside, values * scale, 0.0)


def finish(base, first, got, window, terms):
    whole = pl.BlockSpec(memory_space=pltpu.VMEM)
    return pl.pallas_call(
        functools.partial(finish_kernel, window, terms),
        in_specs=[pl.BlockSpec(memory_space=pltpu.SMEM), whole, whole],
        out_specs=whole,
        out_shape=jax.ShapeDtypeStruct((got.shape[2], NY * (got.shape[1] - 8)), jnp.float32),
        compiler_params=pltpu.CompilerParams(vmem_limit_bytes=VMEM_LIMIT),
    )(base, first[:, None], got)


def fence(*arrays):
    return lax.optimization_barrier(arrays)


def shards(train_grads, left_factor, right_factor, queries, owners, range_start):
    highest = lax.Precision.HIGHEST
    nmods = lax.axis_size("mod")
    nblk = lax.axis_size("blk")
    rows_dev = train_grads.shape[1]
    feat = train_grads.shape[2]
    side = left_factor.shape[1]
    qblock = queries.shape[1]
    half = qblock // 2
    window = rows_dev * nblk // 2
    grads = train_grads[0]
    m = lax.axis_index("mod")
    b = lax.axis_index("blk")
    z, h, c = b // 4, (b // 2) % 2, b % 2

    mats = queries[0].reshape(qblock, side, side)
    mats = jnp.einsum("rad,cd->rac", mats, right_factor[0], precision=highest)
    mats = jnp.einsum("ba,rac->rbc", left_factor[0], mats, precision=highest)
    own = mats.reshape(qblock, feat)

    own, grads = fence(own, grads)
    halves = []

    def ids(*named):
        for flip in range(2):
            for d, col, *ps in named:
                where = (z + d) % NZ * 4 + (h + col) % 2 * 2 + (c + flip) % 2
                halves.extend(where * 2 + p for p in (ps or (0, 1)))

    size = qblock
    a1m, a1p, e0 = up(own), down(own), far(own)
    a1m, a1p = fence(a1m, a1p)
    a2m, a2p, e1p = up(a1m), down(a1p), far(a1p)
    hi, lo, squares = split_grads(grads)
    a2m, a2p, e0, hi, lo, squares = fence(a2m, a2p, e0, hi, lo, squares)
    a3m, a3p, e1m = up(a2m), down(a2p), far(a1m)
    (near,) = pack([own, a1m, a1p, e0, a2m, a2p], [(k, 0, size) for k in range(6)])
    near_c = other(near)
    ids((0, 0), (-1, 0), (1, 0), (0, 1), (-2, 0), (2, 0))
    part0 = scores_of((hi, lo), [(near, 0, 6 * size), (near_c, 0, 6 * size)], squares)
    a3m, a3p, e1m, e1p, part0 = fence(a3m, a3p, e1m, e1p, part0)
    for_up, for_down, for_far, three = pack(
        [a3m, a3p, e1m, e1p],
        [(0, 0, half), (2, 0, half)],
        [(1, half, half), (3, 0, half)],
        [(1, half, half), (0, half, half)],
        [(k, 0, size) for k in range(4)],
    )
    up4, down4, far4 = up(for_up), down(for_down), far(for_far)
    three_c, part0 = fence(other(three), part0)
    got0 = over_y(part0)
    ids((-3, 0), (3, 0), (-1, 1), (1, 1))
    part1 = scores_of((hi, lo), [(three, 0, 4 * size), (three_c, 0, 4 * size)])
    up4, down4, far4, part1 = fence(up4, down4, far4, part1)
    for_up, for_down, for_far, four = pack(
        [up4, down4, far4, e1m, e1p],
        [(3, half, half), (0, half, half)],
        [(4, half, half), (1, half, half)],
        [(0, 0, half), (1, 0, half)],
        [(k, 0, size) for k in range(3)],
    )
    up5, down5, far5 = up(for_up), down(for_down), far(for_far)
    four_c, part1 = fence(other(four), part1)
    got1 = over_y(part1)
    ids((4, 0, 0), (-2, 1, 0), (4, 0, 1), (2, 1, 0))
    part2 = scores_of((hi, lo), [(four, 0, 2 * size), (four_c, 0, 2 * size)])
    up5, down5, far5, part2, got0 = fence(up5, down5, far5, part2, got0)
    (five,) = pack([up5, down5, far5], [(k, 0, size) for k in range(3)])
    five_c = other(five)
    got2 = over_y(part2)
    ids((3, 1, 1), (-3, 1, 1), (-2, 1, 1), (-3, 1, 0), (2, 1, 1), (3, 1, 0), (4, 1, 0), (4, 1, 1))
    part3 = scores_of(
        (hi, lo),
        [(four, 2 * size, size), (five, 0, 3 * size), (four_c, 2 * size, size), (five_c, 0, 3 * size)],
    )
    part3, got1 = fence(part3, got1)
    got3 = over_y(part3)

    source = jnp.stack(halves).astype(jnp.int32)
    blocks = jnp.arange(nblk, dtype=jnp.int32)
    target = jnp.sum(jnp.where((source // 2)[:, None] == blocks[None, :], owners[None, :], 0), axis=1)
    dest = ((target * 2 + source % 2) * half)[:, None] + jnp.arange(half, dtype=jnp.int32)[None, :]
    dest = dest.reshape(-1)
    placed = place(dest, [got0, got1, got2, got3])
    got = lax.all_to_all(placed, "mod", 0, 0)
    out_block = m * (nblk // nmods) + jnp.arange(placed.shape[2], dtype=jnp.int32) // qblock
    first = jnp.sum(jnp.where(out_block[:, None] == blocks[None, :], range_start[None, :], 0), axis=1)
    base = jnp.reshape(b * rows_dev, (1,)).astype(jnp.int32)
    return finish(base, first, got, window, nmods * feat)


def solution(mesh):
    in_specs = (
        P("mod", "blk", None),
        P("mod", None, None),
        P("mod", None, None),
        P("mod", "blk", None),
        P(),
        P(),
    )
    out_specs = P("mod", "blk")
    return jax.shard_map(shards, mesh=mesh, in_specs=in_specs, out_specs=out_specs, check_vma=False)
```

```python
import functools

import jax
import jax.numpy as jnp
from jax import lax
from jax.experimental import pallas as pl
from jax.experimental.pallas import tpu as pltpu
from jax.sharding import PartitionSpec as P

NZ = 8
NY = 4
FEAT_STEP = 512
VMEM_LIMIT = 16 * 1024 * 1024


def blk_pairs(move):
    return [
        (z * 4 + h * 2 + c, move(z, h, c))
        for z in range(NZ)
        for h in range(2)
        for c in range(2)
    ]


Z_UP = blk_pairs(lambda z, h, c: (z + 1) % NZ * 4 + h * 2 + c)
Z_DOWN = blk_pairs(lambda z, h, c: (z - 1) % NZ * 4 + h * 2 + c)
X_FAR = blk_pairs(lambda z, h, c: z * 4 + (1 - h) * 2 + c)
CORE = blk_pairs(lambda z, h, c: z * 4 + h * 2 + 1 - c)
Y_GROUPS = [[x * 4 + y for y in range(NY)] for x in range(2)]


def up(block):
    return lax.ppermute(block, "blk", Z_UP)


def down(block):
    return lax.ppermute(block, "blk", Z_DOWN)


def far(block):
    return lax.ppermute(block, "blk", X_FAR)


def other(block):
    return lax.ppermute(block, "blk", CORE)


def split(value):
    high = value.astype(jnp.bfloat16)
    low = (value - high.astype(jnp.float32)).astype(jnp.bfloat16)
    return high, low


def nt(a, b):
    return lax.dot_general(a, b, (((1,), (1,)), ((), ())), preferred_element_type=jnp.float32)


def split_kernel(g_ref, hi_ref, lo_ref, sq_ref):
    g = g_ref[...]
    high, low = split(g)
    for k in range(hi_ref.shape[0]):
        part = slice(k * FEAT_STEP, (k + 1) * FEAT_STEP)
        hi_ref[k], lo_ref[k] = high[:, part], low[:, part]
    sq_ref[...] = jnp.broadcast_to(jnp.sum(g * g, axis=1, keepdims=True), sq_ref.shape)


def split_grads(grads):
    rows, feat = grads.shape
    steps = feat // FEAT_STEP
    piece = pl.BlockSpec((steps, 64, FEAT_STEP), lambda i: (0, i, 0))
    return pl.pallas_call(
        split_kernel,
        grid=(rows // 64,),
        in_specs=[pl.BlockSpec((64, feat), lambda i: (i, 0))],
        out_specs=[piece, piece, pl.BlockSpec((64, 128), lambda i: (i, 0))],
        out_shape=[
            pltpu.HBM((steps, rows, FEAT_STEP), jnp.bfloat16),
            pltpu.HBM((steps, rows, FEAT_STEP), jnp.bfloat16),
            jax.ShapeDtypeStruct((rows, 128), jnp.float32),
        ],
        compiler_params=pltpu.CompilerParams(vmem_limit_bytes=VMEM_LIMIT),
    )(pltpu.with_memory_space_constraint(grads, pltpu.HBM))


def score_kernel(spans, squares, hi_ref, lo_ref, *refs):
    if squares:
        sq_ref, *refs = refs
    pieces = refs[: len(spans)]
    out_ref, acc = refs[len(spans) :]
    step = pl.program_id(0)
    rows = acc.shape[0]
    q = jnp.concatenate([p[a:b, :] for p, (a, b) in zip(pieces, spans)], axis=0)
    qhi, qlo = split(q)
    ghi, glo = hi_ref[0], lo_ref[0]
    value = nt(ghi, qhi) + (nt(ghi, qlo) + nt(glo, qhi))

    @pl.when(step == 0)
    def _():
        acc[...] = value

    @pl.when(step > 0)
    def _():
        acc[...] += value

    @pl.when(step == pl.num_programs(0) - 1)
    def _():
        emit(squares, sq_ref if squares else None, acc, out_ref)


def emit(squares, sq_ref, acc, out_ref):
    rows = acc.shape[0]
    count = rows // NY
    for k in range(NY):
        here = slice(k * count, (k + 1) * count)
        out_ref[k, 0:count, :] = acc[here, :]
        if squares:
            out_ref[k, count:, :] = jnp.zeros((8, out_ref.shape[2]), jnp.float32)
            out_ref[k, count:, 0:count] = jnp.transpose(sq_ref[here, 0:8])


def scores_of(grads, pieces, squares=None):
    hi, lo = (pltpu.with_memory_space_constraint(g, pltpu.HBM) for g in grads)
    steps, rows, wide = hi.shape
    spans = [(first, first + count) for _, first, count in pieces]
    width = sum(count for _, _, count in pieces)
    slice_rows = rows // NY + (0 if squares is None else 8)
    whole = pl.BlockSpec(memory_space=pltpu.VMEM)
    extra = [] if squares is None else [squares]
    flops = 6 * rows * width * steps * wide
    return pl.pallas_call(
        functools.partial(score_kernel, spans, squares is not None),
        grid=(steps,),
        in_specs=[pl.BlockSpec((1, rows, wide), lambda i: (i, 0, 0))] * 2
        + [whole] * len(extra)
        + [pl.BlockSpec((p[0].shape[0], wide), lambda i: (0, i)) for p in pieces],
        out_specs=whole,
        out_shape=jax.ShapeDtypeStruct((NY, slice_rows, width), jnp.float32),
        scratch_shapes=[pltpu.VMEM((rows, width), jnp.float32)],
        compiler_params=pltpu.CompilerParams(vmem_limit_bytes=VMEM_LIMIT),
        cost_estimate=pl.CostEstimate(flops=flops, bytes_accessed=4 * 1024 * 1024, transcendentals=0),
    )(hi, lo, *extra, *[p[0] for p in pieces])


def over_y(slices):
    return lax.all_to_all(slices, "mod", 0, 0, axis_index_groups=Y_GROUPS)


def pack_kernel(plans, *refs):
    blocks, outs = refs[: -len(plans)], refs[-len(plans) :]
    for out, plan in zip(outs, plans):
        at = 0
        for which, first, count in plan:
            out[at : at + count, :] = blocks[which][first : first + count, :]
            at += count


def pack(blocks, *plans):
    whole = pl.BlockSpec(memory_space=pltpu.VMEM)
    return pl.pallas_call(
        functools.partial(pack_kernel, plans),
        in_specs=[whole] * len(blocks),
        out_specs=[whole] * len(plans),
        out_shape=[
            jax.ShapeDtypeStruct((sum(p[2] for p in plan), blocks[0].shape[1]), jnp.float32)
            for plan in plans
        ],
        compiler_params=pltpu.CompilerParams(vmem_limit_bytes=VMEM_LIMIT),
    )(*blocks)


def place_kernel(dest_ref, *refs):
    *parts, out_ref = refs
    sums = [p[0] + p[1] + (p[2] + p[3]) for p in parts]
    count = parts[-1].shape[1]
    total = jnp.concatenate([v[:count] for v in sums], axis=1)
    high = total.astype(jnp.bfloat16)
    rest = total - high.astype(jnp.float32)
    mid = rest.astype(jnp.bfloat16)
    low = (rest - mid.astype(jnp.float32)).astype(jnp.bfloat16)
    stacked = jnp.concatenate([high, mid, low], axis=0)
    squares = sums[0][count:, :]
    row = lax.broadcasted_iota(jnp.int32, (8, 128), 0)
    tail = jnp.where(row == 0, squares[:, 0:128], squares[:, 128:256])
    nq = dest_ref.shape[0]
    lane = lax.broadcasted_iota(jnp.int32, (nq, 256), 1)
    for first in range(0, nq, 256):
        pick = jnp.where(dest_ref[...] == lane + first, 1.0, 0.0).astype(jnp.bfloat16)
        moved = jnp.dot(stacked, pick, preferred_element_type=jnp.float32)
        moved = moved[:count] + (moved[count : 2 * count] + moved[2 * count :])
        for k in range(2):
            out_ref[first // 128 + k, 0:count, :] = moved[:, k * 128 : (k + 1) * 128]
            out_ref[first // 128 + k, count:, :] = tail


def place(dest, parts):
    whole = pl.BlockSpec(memory_space=pltpu.VMEM)
    nq = dest.shape[0]
    return pl.pallas_call(
        place_kernel,
        in_specs=[whole] * (1 + len(parts)),
        out_specs=whole,
        out_shape=jax.ShapeDtypeStruct((nq // 128, parts[0].shape[1], 128), jnp.float32),
        compiler_params=pltpu.CompilerParams(vmem_limit_bytes=VMEM_LIMIT),
    )(dest[:, None], *parts)


def finish_kernel(window, terms, base_ref, first_ref, got_ref, out_ref):
    rows = got_ref.shape[1] - 8
    both = [got_ref[k] + got_ref[NY + k] for k in range(NY)]
    values = jnp.transpose(jnp.concatenate([v[:rows] for v in both], axis=0))
    squares = jnp.concatenate(
        [w for v in both for w in (v[rows : rows + 1, :], v[rows + 1 : rows + 2, : rows - 128])],
        axis=1,
    )
    scale = lax.rsqrt(squares / terms + 1e-06)
    ids = base_ref[0] + lax.broadcasted_iota(jnp.int32, values.shape, 1)
    first = first_ref[...]
    inside = (ids >= first) & (ids < first + window)
    out_ref[...] = jnp.where(inside, values * scale, 0.0)


def finish(base, first, got, window, terms):
    whole = pl.BlockSpec(memory_space=pltpu.VMEM)
    return pl.pallas_call(
        functools.partial(finish_kernel, window, terms),
        in_specs=[pl.BlockSpec(memory_space=pltpu.SMEM), whole, whole],
        out_specs=whole,
        out_shape=jax.ShapeDtypeStruct((got.shape[2], NY * (got.shape[1] - 8)), jnp.float32),
        compiler_params=pltpu.CompilerParams(vmem_limit_bytes=VMEM_LIMIT),
    )(base, first[:, None], got)


def fence(*arrays):
    return lax.optimization_barrier(arrays)


def shards(train_grads, left_factor, right_factor, queries, owners, range_start):
    highest = lax.Precision.HIGHEST
    nmods = lax.axis_size("mod")
    nblk = lax.axis_size("blk")
    rows_dev = train_grads.shape[1]
    feat = train_grads.shape[2]
    side = left_factor.shape[1]
    qblock = queries.shape[1]
    half = qblock // 2
    window = rows_dev * nblk // 2
    grads = train_grads[0]
    m = lax.axis_index("mod")
    b = lax.axis_index("blk")
    z, h, c = b // 4, (b // 2) % 2, b % 2

    mats = queries[0].reshape(qblock, side, side)
    mats = jnp.einsum("rad,cd->rac", mats, right_factor[0], precision=highest)
    mats = jnp.einsum("ba,rac->rbc", left_factor[0], mats, precision=highest)
    own = mats.reshape(qblock, feat)

    own, grads = fence(own, grads)
    halves = []

    def ids(*named):
        for flip in range(2):
            for d, col, *ps in named:
                where = (z + d) % NZ * 4 + (h + col) % 2 * 2 + (c + flip) % 2
                halves.extend(where * 2 + p for p in (ps or (0, 1)))

    size = qblock
    a1m, a1p, e0 = up(own), down(own), far(own)
    a1m, a1p = fence(a1m, a1p)
    a2m, a2p, e1p = up(a1m), down(a1p), far(a1p)
    hi, lo, squares = split_grads(grads)
    a2m, a2p, e0, e1p, squares = fence(a2m, a2p, e0, e1p, squares)
    a3m, a3p, e1m = up(a2m), down(a2p), far(a1m)
    (near,) = pack([own, a1m, a1p, e0, a2m, a2p], [(k, 0, size) for k in range(6)])
    near_c = other(near)
    ids((0, 0), (-1, 0), (1, 0), (0, 1), (-2, 0), (2, 0))
    part0 = scores_of((hi, lo), [(near, 0, 6 * size), (near_c, 0, 6 * size)], squares)
    a3m, a3p, e1m, part0 = fence(a3m, a3p, e1m, part0)
    for_up, for_down, for_far, three = pack(
        [a3m, a3p, e1m, e1p],
        [(0, 0, half), (2, 0, half)],
        [(1, half, half), (3, 0, half)],
        [(1, half, half), (0, half, half)],
        [(k, 0, size) for k in range(4)],
    )
    up4, down4, far4 = up(for_up), down(for_down), far(for_far)
    three_c, part0 = fence(other(three), part0)
    got0 = over_y(part0)
    ids((-3, 0), (3, 0), (-1, 1), (1, 1))
    part1 = scores_of((hi, lo), [(three, 0, 4 * size), (three_c, 0, 4 * size)])
    up4, down4, far4, part1 = fence(up4, down4, far4, part1)
    for_up, for_down, for_far, four = pack(
        [up4, down4, far4, e1m, e1p],
        [(3, half, half), (0, half, half)],
        [(4, half, half), (1, half, half)],
        [(0, 0, half), (1, 0, half)],
        [(k, 0, size) for k in range(3)],
    )
    up5, down5, far5 = up(for_up), down(for_down), far(for_far)
    four_c, part1 = fence(other(four), part1)
    got1 = over_y(part1)
    ids((4, 0, 0), (-2, 1, 0), (4, 0, 1), (2, 1, 0))
    part2 = scores_of((hi, lo), [(four, 0, 2 * size), (four_c, 0, 2 * size)])
    up5, down5, far5, part2, got1 = fence(up5, down5, far5, part2, got1)
    (five,) = pack([up5, down5, far5], [(k, 0, size) for k in range(3)])
    five_c = other(five)
    got2 = over_y(part2)
    ids((3, 1, 1), (-3, 1, 1), (-2, 1, 1), (-3, 1, 0), (2, 1, 1), (3, 1, 0), (4, 1, 0), (4, 1, 1))
    part3 = scores_of(
        (hi, lo),
        [(four, 2 * size, size), (five, 0, 3 * size), (four_c, 2 * size, size), (five_c, 0, 3 * size)],
    )
    part3, got2 = fence(part3, got2)
    got3 = over_y(part3)

    source = jnp.stack(halves).astype(jnp.int32)
    blocks = jnp.arange(nblk, dtype=jnp.int32)
    target = jnp.sum(jnp.where((source // 2)[:, None] == blocks[None, :], owners[None, :], 0), axis=1)
    dest = ((target * 2 + source % 2) * half)[:, None] + jnp.arange(half, dtype=jnp.int32)[None, :]
    dest = dest.reshape(-1)
    placed = place(dest, [got0, got1, got2, got3])
    got = lax.all_to_all(placed, "mod", 0, 0)
    out_block = m * (nblk // nmods) + jnp.arange(placed.shape[2], dtype=jnp.int32) // qblock
    first = jnp.sum(jnp.where(out_block[:, None] == blocks[None, :], range_start[None, :], 0), axis=1)
    base = jnp.reshape(b * rows_dev, (1,)).astype(jnp.int32)
    return finish(base, first, got, window, nmods * feat)


def solution(mesh):
    in_specs = (
        P("mod", "blk", None),
        P("mod", None, None),
        P("mod", None, None),
        P("mod", "blk", None),
        P(),
        P(),
    )
    out_specs = P("mod", "blk")
    return jax.shard_map(shards, mesh=mesh, in_specs=in_specs, out_specs=out_specs, check_vma=False)
```

```python
import functools

import jax
import jax.numpy as jnp
from jax import lax
from jax.experimental import pallas as pl
from jax.experimental.pallas import tpu as pltpu
from jax.sharding import PartitionSpec as P

NZ = 8
NY = 4
FEAT_STEP = 1024
VMEM_LIMIT = 16 * 1024 * 1024


def blk_pairs(move):
    return [
        (z * 4 + h * 2 + c, move(z, h, c))
        for z in range(NZ)
        for h in range(2)
        for c in range(2)
    ]


Z_UP = blk_pairs(lambda z, h, c: (z + 1) % NZ * 4 + h * 2 + c)
Z_DOWN = blk_pairs(lambda z, h, c: (z - 1) % NZ * 4 + h * 2 + c)
X_FAR = blk_pairs(lambda z, h, c: z * 4 + (1 - h) * 2 + c)
CORE = blk_pairs(lambda z, h, c: z * 4 + h * 2 + 1 - c)
Y_GROUPS = [[x * 4 + y for y in range(NY)] for x in range(2)]


def up(block):
    return lax.ppermute(block, "blk", Z_UP)


def down(block):
    return lax.ppermute(block, "blk", Z_DOWN)


def far(block):
    return lax.ppermute(block, "blk", X_FAR)


def other(block):
    return lax.ppermute(block, "blk", CORE)


def split(value):
    high = value.astype(jnp.bfloat16)
    low = (value - high.astype(jnp.float32)).astype(jnp.bfloat16)
    return high, low


def nt(a, b):
    return lax.dot_general(a, b, (((1,), (1,)), ((), ())), preferred_element_type=jnp.float32)


def split_kernel(g_ref, hi_ref, lo_ref, sq_ref):
    g = g_ref[...]
    high, low = split(g)
    for k in range(hi_ref.shape[0]):
        part = slice(k * FEAT_STEP, (k + 1) * FEAT_STEP)
        hi_ref[k], lo_ref[k] = high[:, part], low[:, part]
    sq_ref[...] = jnp.broadcast_to(jnp.sum(g * g, axis=1, keepdims=True), sq_ref.shape)


def split_grads(grads):
    rows, feat = grads.shape
    steps = feat // FEAT_STEP
    piece = pl.BlockSpec((steps, 64, FEAT_STEP), lambda i: (0, i, 0))
    return pl.pallas_call(
        split_kernel,
        grid=(rows // 64,),
        in_specs=[pl.BlockSpec((64, feat), lambda i: (i, 0))],
        out_specs=[piece, piece, pl.BlockSpec((64, 128), lambda i: (i, 0))],
        out_shape=[
            pltpu.HBM((steps, rows, FEAT_STEP), jnp.bfloat16),
            pltpu.HBM((steps, rows, FEAT_STEP), jnp.bfloat16),
            jax.ShapeDtypeStruct((rows, 128), jnp.float32),
        ],
        compiler_params=pltpu.CompilerParams(vmem_limit_bytes=VMEM_LIMIT),
    )(pltpu.with_memory_space_constraint(grads, pltpu.HBM))


def score_kernel(spans, squares, prior, hi_ref, lo_ref, *refs):
    sq_ref = old_ref = None
    if squares:
        sq_ref, *refs = refs
    if prior:
        old_ref, *refs = refs
    pieces = refs[: len(spans)]
    out_ref, acc = refs[len(spans) :]
    step = pl.program_id(0)
    rows = acc.shape[0]
    q = jnp.concatenate([p[a:b, :] for p, (a, b) in zip(pieces, spans)], axis=0)
    qhi, qlo = split(q)
    ghi, glo = hi_ref[0], lo_ref[0]
    value = nt(ghi, qhi) + (nt(ghi, qlo) + nt(glo, qhi))

    @pl.when(step == 0)
    def _():
        acc[...] = value

    @pl.when(step > 0)
    def _():
        acc[...] += value

    @pl.when(step == pl.num_programs(0) - 1)
    def _():
        emit(sq_ref, old_ref, acc, out_ref)


def emit(sq_ref, old_ref, acc, out_ref):
    count = acc.shape[0] // NY
    at = out_ref.shape[2] - acc.shape[1]
    for k in range(NY):
        here = slice(k * count, (k + 1) * count)
        out_ref[k, 0:count, at:] = acc[here, :]
        if old_ref is not None:
            out_ref[k, :, 0:at] = old_ref[k]
            out_ref[k, count:, at:] = jnp.zeros((out_ref.shape[1] - count, acc.shape[1]), jnp.float32)
        if sq_ref is not None:
            out_ref[k, count:, :] = jnp.zeros((8, out_ref.shape[2]), jnp.float32)
            out_ref[k, count:, 0:count] = jnp.transpose(sq_ref[here, 0:8])


def scores_of(grads, pieces, squares=None, prior=None):
    hi, lo = (pltpu.with_memory_space_constraint(g, pltpu.HBM) for g in grads)
    steps, rows, wide = hi.shape
    spans = [(first, first + count) for _, first, count in pieces]
    width = sum(count for _, _, count in pieces)
    slice_rows = rows // NY + (0 if squares is None else 8)
    if prior is not None:
        slice_rows = prior.shape[1]
    whole = pl.BlockSpec(memory_space=pltpu.VMEM)
    extra = [v for v in (squares, prior) if v is not None]
    full = width + (0 if prior is None else prior.shape[2])
    flops = 6 * rows * width * steps * wide
    return pl.pallas_call(
        functools.partial(score_kernel, spans, squares is not None, prior is not None),
        grid=(steps,),
        in_specs=[pl.BlockSpec((1, rows, wide), lambda i: (i, 0, 0))] * 2
        + [whole] * len(extra)
        + [pl.BlockSpec((p[0].shape[0], wide), lambda i: (0, i)) for p in pieces],
        out_specs=whole,
        out_shape=jax.ShapeDtypeStruct((NY, slice_rows, full), jnp.float32),
        scratch_shapes=[pltpu.VMEM((rows, width), jnp.float32)],
        compiler_params=pltpu.CompilerParams(vmem_limit_bytes=VMEM_LIMIT),
        cost_estimate=pl.CostEstimate(flops=flops, bytes_accessed=4 * 1024 * 1024, transcendentals=0),
    )(hi, lo, *extra, *[p[0] for p in pieces])


def over_y(slices):
    return lax.all_to_all(slices, "mod", 0, 0, axis_index_groups=Y_GROUPS)


def pack_kernel(plans, *refs):
    blocks, outs = refs[: -len(plans)], refs[-len(plans) :]
    for out, plan in zip(outs, plans):
        at = 0
        for which, first, count in plan:
            out[at : at + count, :] = blocks[which][first : first + count, :]
            at += count


def pack(blocks, *plans):
    whole = pl.BlockSpec(memory_space=pltpu.VMEM)
    return pl.pallas_call(
        functools.partial(pack_kernel, plans),
        in_specs=[whole] * len(blocks),
        out_specs=[whole] * len(plans),
        out_shape=[
            jax.ShapeDtypeStruct((sum(p[2] for p in plan), blocks[0].shape[1]), jnp.float32)
            for plan in plans
        ],
        compiler_params=pltpu.CompilerParams(vmem_limit_bytes=VMEM_LIMIT),
    )(*blocks)


def place_kernel(nparts, dest_ref, *refs):
    parts, (*old, out_ref) = refs[:nparts], refs[nparts:]
    sums = [p[0] + p[1] + (p[2] + p[3]) for p in parts]
    count = parts[-1].shape[1]
    total = jnp.concatenate([v[:count] for v in sums], axis=1)
    high = total.astype(jnp.bfloat16)
    rest = total - high.astype(jnp.float32)
    mid = rest.astype(jnp.bfloat16)
    low = (rest - mid.astype(jnp.float32)).astype(jnp.bfloat16)
    stacked = jnp.concatenate([high, mid, low], axis=0)
    if old:
        tail = old[0][0, count:, :]
    else:
        squares = sums[0][count:, :]
        row = lax.broadcasted_iota(jnp.int32, (8, 128), 0)
        tail = jnp.where(row == 0, squares[:, 0:128], squares[:, 128:256])
    slot = lax.broadcasted_iota(jnp.int32, (256, total.shape[1]), 0)
    for first in range(0, 128 * out_ref.shape[0], 256):
        pick = jnp.where(dest_ref[...] == slot + first, 1.0, 0.0).astype(jnp.bfloat16)
        moved = nt(stacked, pick)
        moved = moved[:count] + (moved[count : 2 * count] + moved[2 * count :])
        for k in range(2):
            at = first // 128 + k
            value = moved[:, k * 128 : (k + 1) * 128]
            out_ref[at, 0:count, :] = value + old[0][at, 0:count, :] if old else value
            out_ref[at, count:, :] = tail


def place(groups, dest, parts, rows, old=()):
    whole = pl.BlockSpec(memory_space=pltpu.VMEM)
    return pl.pallas_call(
        functools.partial(place_kernel, len(parts)),
        grid=(1,),
        in_specs=[whole] * (1 + len(parts) + len(old)),
        out_specs=whole,
        out_shape=jax.ShapeDtypeStruct((groups, rows, 128), jnp.float32),
        compiler_params=pltpu.CompilerParams(vmem_limit_bytes=VMEM_LIMIT),
        cost_estimate=pl.CostEstimate(flops=10**9, bytes_accessed=4 * 1024 * 1024, transcendentals=0),
    )(dest[None, :], *parts, *old)


def finish_kernel(window, terms, base_ref, first_ref, got_ref, out_ref):
    rows = got_ref.shape[1] - 8
    both = [got_ref[k] + got_ref[NY + k] for k in range(NY)]
    values = jnp.transpose(jnp.concatenate([v[:rows] for v in both], axis=0))
    squares = jnp.concatenate(
        [w for v in both for w in (v[rows : rows + 1, :], v[rows + 1 : rows + 2, : rows - 128])],
        axis=1,
    )
    scale = lax.rsqrt(squares / terms + 1e-06)
    ids = base_ref[0] + lax.broadcasted_iota(jnp.int32, values.shape, 1)
    first = first_ref[...]
    inside = (ids >= first) & (ids < first + window)
    out_ref[...] = jnp.where(inside, values * scale, 0.0)


def finish(base, first, got, window, terms):
    whole = pl.BlockSpec(memory_space=pltpu.VMEM)
    return pl.pallas_call(
        functools.partial(finish_kernel, window, terms),
        in_specs=[pl.BlockSpec(memory_space=pltpu.SMEM), whole, whole],
        out_specs=whole,
        out_shape=jax.ShapeDtypeStruct((got.shape[2], NY * (got.shape[1] - 8)), jnp.float32),
        compiler_params=pltpu.CompilerParams(vmem_limit_bytes=VMEM_LIMIT),
    )(base, first[:, None], got)


def fence(*arrays):
    return lax.optimization_barrier(arrays)


def shards(train_grads, left_factor, right_factor, queries, owners, range_start):
    highest = lax.Precision.HIGHEST
    nmods = lax.axis_size("mod")
    nblk = lax.axis_size("blk")
    rows_dev = train_grads.shape[1]
    feat = train_grads.shape[2]
    side = left_factor.shape[1]
    qblock = queries.shape[1]
    half = qblock // 2
    window = rows_dev * nblk // 2
    grads = train_grads[0]
    m = lax.axis_index("mod")
    b = lax.axis_index("blk")
    z, h, c = b // 4, (b // 2) % 2, b % 2

    mats = queries[0].reshape(qblock, side, side)
    mats = jnp.einsum("rad,cd->rac", mats, right_factor[0], precision=highest)
    mats = jnp.einsum("ba,rac->rbc", left_factor[0], mats, precision=highest)
    own = mats.reshape(qblock, feat)

    own, grads = fence(own, grads)
    halves = []

    def ids(*named):
        for flip in range(2):
            for d, col, *ps in named:
                where = (z + d) % NZ * 4 + (h + col) % 2 * 2 + (c + flip) % 2
                halves.extend(where * 2 + p for p in (ps or (0, 1)))

    size = qblock
    a1m, a1p, e0 = up(own), down(own), far(own)
    a1m, a1p = fence(a1m, a1p)
    a2m, a2p, e1p = up(a1m), down(a1p), far(a1p)
    hi, lo, squares = split_grads(grads)
    a2m, a2p, e0, e1p, squares = fence(a2m, a2p, e0, e1p, squares)
    a3m, a3p, e1m = up(a2m), down(a2p), far(a1m)
    (near,) = pack([own, a1m, a1p, e0, a2m, a2p], [(k, 0, size) for k in range(6)])
    near_c = other(near)
    ids((0, 0), (-1, 0), (1, 0), (0, 1), (-2, 0), (2, 0))
    part0 = scores_of((hi, lo), [(near, 0, 6 * size), (near_c, 0, 6 * size)], squares)
    a3m, a3p, e1m, part0 = fence(a3m, a3p, e1m, part0)
    for_up, for_down, for_far, three = pack(
        [a3m, a3p, e1m, e1p],
        [(0, 0, half), (2, 0, half)],
        [(1, half, half), (3, 0, half)],
        [(1, half, half), (0, half, half)],
        [(k, 0, size) for k in range(4)],
    )
    up4, down4, far4 = up(for_up), down(for_down), far(for_far)
    three_c = other(three)
    ids((-3, 0), (3, 0), (-1, 1), (1, 1))
    part1 = scores_of((hi, lo), [(three, 0, 4 * size), (three_c, 0, 4 * size)])
    up4, down4, far4, part1 = fence(up4, down4, far4, part1)
    for_up, for_down, for_far, four = pack(
        [up4, down4, far4, e1m, e1p],
        [(3, half, half), (0, half, half)],
        [(4, half, half), (1, half, half)],
        [(0, 0, half), (1, 0, half)],
        [(k, 0, size) for k in range(3)],
    )
    up5, down5, far5 = up(for_up), down(for_down), far(for_far)
    four_c, part1 = fence(other(four), part1)
    got1 = over_y(part1)
    ids((4, 0, 0), (-2, 1, 0), (4, 0, 1), (2, 1, 0))
    part02 = scores_of((hi, lo), [(four, 0, 2 * size), (four_c, 0, 2 * size)], prior=part0)
    up5, down5, far5, part02, got1 = fence(up5, down5, far5, part02, got1)
    (five,) = pack([up5, down5, far5], [(k, 0, size) for k in range(3)])
    five_c = other(five)
    got02 = over_y(part02)
    ids((3, 1, 1), (-3, 1, 1), (-2, 1, 1), (-3, 1, 0), (2, 1, 1), (3, 1, 0), (4, 1, 0), (4, 1, 1))
    part3 = scores_of(
        (hi, lo),
        [(four, 2 * size, size), (five, 0, 3 * size), (four_c, 2 * size, size), (five_c, 0, 3 * size)],
    )
    part3, got02 = fence(part3, got02)
    got3 = over_y(part3)

    source = jnp.stack(halves).astype(jnp.int32)
    blocks = jnp.arange(nblk, dtype=jnp.int32)
    target = jnp.sum(jnp.where((source // 2)[:, None] == blocks[None, :], owners[None, :], 0), axis=1)
    dest = ((target * 2 + source % 2) * half)[:, None] + jnp.arange(half, dtype=jnp.int32)[None, :]
    dest = dest.reshape(-1)
    ends = (part0.shape[2], part0.shape[2] + part1.shape[2], part02.shape[2] + part1.shape[2])
    early = ends[2]
    first_dest = jnp.concatenate([dest[: ends[0]], dest[ends[1] : early], dest[ends[0] : ends[1]]])
    groups, rows = dest.shape[0] // 128, got02.shape[1]
    placed = place(groups, first_dest, [got02, got1], rows)
    placed = place(groups, dest[early:], [got3], rows, [placed])
    got = lax.all_to_all(placed, "mod", 0, 0)
    out_block = m * (nblk // nmods) + jnp.arange(placed.shape[2], dtype=jnp.int32) // qblock
    first = jnp.sum(jnp.where(out_block[:, None] == blocks[None, :], range_start[None, :], 0), axis=1)
    base = jnp.reshape(b * rows_dev, (1,)).astype(jnp.int32)
    return finish(base, first, got, window, nmods * feat)


def solution(mesh):
    in_specs = (
        P("mod", "blk", None),
        P("mod", None, None),
        P("mod", None, None),
        P("mod", "blk", None),
        P(),
        P(),
    )
    out_specs = P("mod", "blk")
    return jax.shard_map(shards, mesh=mesh, in_specs=in_specs, out_specs=out_specs, check_vma=False)
```

```python
import functools

import jax
import jax.numpy as jnp
from jax import lax
from jax.experimental import pallas as pl
from jax.experimental.pallas import tpu as pltpu
from jax.sharding import PartitionSpec as P

NZ = 8
NY = 4
FEAT_STEP = 1024
VMEM_LIMIT = 16 * 1024 * 1024


def blk_pairs(move):
    return [
        (z * 4 + h * 2 + c, move(z, h, c))
        for z in range(NZ)
        for h in range(2)
        for c in range(2)
    ]


Z_UP = blk_pairs(lambda z, h, c: (z + 1) % NZ * 4 + h * 2 + c)
Z_DOWN = blk_pairs(lambda z, h, c: (z - 1) % NZ * 4 + h * 2 + c)
X_FAR = blk_pairs(lambda z, h, c: z * 4 + (1 - h) * 2 + c)
CORE = blk_pairs(lambda z, h, c: z * 4 + h * 2 + 1 - c)
Y_GROUPS = [[x * 4 + y for y in range(NY)] for x in range(2)]


def up(block):
    return lax.ppermute(block, "blk", Z_UP)


def down(block):
    return lax.ppermute(block, "blk", Z_DOWN)


def far(block):
    return lax.ppermute(block, "blk", X_FAR)


def other(block):
    return lax.ppermute(block, "blk", CORE)


def split(value):
    high = value.astype(jnp.bfloat16)
    low = (value - high.astype(jnp.float32)).astype(jnp.bfloat16)
    return high, low


def nt(a, b):
    return lax.dot_general(a, b, (((1,), (1,)), ((), ())), preferred_element_type=jnp.float32)


def split_kernel(g_ref, hi_ref, lo_ref, sq_ref):
    g = g_ref[...]
    high, low = split(g)
    for k in range(hi_ref.shape[0]):
        part = slice(k * FEAT_STEP, (k + 1) * FEAT_STEP)
        hi_ref[k], lo_ref[k] = high[:, part], low[:, part]
    sq_ref[...] = jnp.broadcast_to(jnp.sum(g * g, axis=1, keepdims=True), sq_ref.shape)


def split_grads(grads):
    rows, feat = grads.shape
    steps = feat // FEAT_STEP
    piece = pl.BlockSpec((steps, 64, FEAT_STEP), lambda i: (0, i, 0))
    return pl.pallas_call(
        split_kernel,
        grid=(rows // 64,),
        in_specs=[pl.BlockSpec((64, feat), lambda i: (i, 0))],
        out_specs=[piece, piece, pl.BlockSpec((64, 128), lambda i: (i, 0))],
        out_shape=[
            pltpu.HBM((steps, rows, FEAT_STEP), jnp.bfloat16),
            pltpu.HBM((steps, rows, FEAT_STEP), jnp.bfloat16),
            jax.ShapeDtypeStruct((rows, 128), jnp.float32),
        ],
        compiler_params=pltpu.CompilerParams(vmem_limit_bytes=VMEM_LIMIT),
    )(pltpu.with_memory_space_constraint(grads, pltpu.HBM))


def score_kernel(spans, squares, hi_ref, lo_ref, *refs):
    sq_ref = None
    if squares:
        sq_ref, *refs = refs
    pieces = refs[: len(spans)]
    out_ref, acc = refs[len(spans) :]
    step = pl.program_id(0)
    rows = acc.shape[0]
    q = jnp.concatenate([p[a:b, :] for p, (a, b) in zip(pieces, spans)], axis=0)
    qhi, qlo = split(q)
    ghi, glo = hi_ref[0], lo_ref[0]
    value = nt(ghi, qhi) + (nt(ghi, qlo) + nt(glo, qhi))

    @pl.when(step == 0)
    def _():
        acc[...] = value

    @pl.when(step > 0)
    def _():
        acc[...] += value

    @pl.when(step == pl.num_programs(0) - 1)
    def _():
        emit(sq_ref, acc, out_ref)


def emit(sq_ref, acc, out_ref):
    count = acc.shape[0] // NY
    for k in range(NY):
        here = slice(k * count, (k + 1) * count)
        out_ref[k, 0:count, :] = acc[here, :]
        if sq_ref is not None:
            out_ref[k, count:, :] = jnp.zeros((8, out_ref.shape[2]), jnp.float32)
            out_ref[k, count:, 0:count] = jnp.transpose(sq_ref[here, 0:8])


def scores_of(grads, pieces, squares=None):
    hi, lo = (pltpu.with_memory_space_constraint(g, pltpu.HBM) for g in grads)
    steps, rows, wide = hi.shape
    spans = [(first, first + count) for _, first, count in pieces]
    width = sum(count for _, _, count in pieces)
    slice_rows = rows // NY + (0 if squares is None else 8)
    whole = pl.BlockSpec(memory_space=pltpu.VMEM)
    extra = [] if squares is None else [squares]
    flops = 6 * rows * width * steps * wide
    return pl.pallas_call(
        functools.partial(score_kernel, spans, squares is not None),
        grid=(steps,),
        in_specs=[pl.BlockSpec((1, rows, wide), lambda i: (i, 0, 0))] * 2
        + [whole] * len(extra)
        + [pl.BlockSpec((p[0].shape[0], wide), lambda i: (0, i)) for p in pieces],
        out_specs=whole,
        out_shape=jax.ShapeDtypeStruct((NY, slice_rows, width), jnp.float32),
        scratch_shapes=[pltpu.VMEM((rows, width), jnp.float32)],
        compiler_params=pltpu.CompilerParams(vmem_limit_bytes=VMEM_LIMIT),
        cost_estimate=pl.CostEstimate(flops=flops, bytes_accessed=4 * 1024 * 1024, transcendentals=0),
    )(hi, lo, *extra, *[p[0] for p in pieces])


def over_y(slices):
    return lax.all_to_all(slices, "mod", 0, 0, axis_index_groups=Y_GROUPS)


def pack_kernel(plans, *refs):
    blocks, outs = refs[: -len(plans)], refs[-len(plans) :]
    for out, plan in zip(outs, plans):
        at = 0
        for which, first, count in plan:
            out[at : at + count, :] = blocks[which][first : first + count, :]
            at += count


def pack(blocks, *plans):
    whole = pl.BlockSpec(memory_space=pltpu.VMEM)
    return pl.pallas_call(
        functools.partial(pack_kernel, plans),
        in_specs=[whole] * len(blocks),
        out_specs=[whole] * len(plans),
        out_shape=[
            jax.ShapeDtypeStruct((sum(p[2] for p in plan), blocks[0].shape[1]), jnp.float32)
            for plan in plans
        ],
        compiler_params=pltpu.CompilerParams(vmem_limit_bytes=VMEM_LIMIT),
    )(*blocks)


def place_kernel(nparts, dest_ref, *refs):
    parts, (*old, out_ref) = refs[:nparts], refs[nparts:]
    sums = [p[0] + p[1] + (p[2] + p[3]) for p in parts]
    count = parts[-1].shape[1]
    total = jnp.concatenate([v[:count] for v in sums], axis=1)
    high = total.astype(jnp.bfloat16)
    rest = total - high.astype(jnp.float32)
    mid = rest.astype(jnp.bfloat16)
    low = (rest - mid.astype(jnp.float32)).astype(jnp.bfloat16)
    stacked = jnp.concatenate([high, mid, low], axis=0)
    if old:
        tail = old[0][0, count:, :]
    else:
        squares = sums[0][count:, :]
        row = lax.broadcasted_iota(jnp.int32, (8, 128), 0)
        tail = jnp.where(row == 0, squares[:, 0:128], squares[:, 128:256])
    slot = lax.broadcasted_iota(jnp.int32, (256, total.shape[1]), 0)
    for first in range(0, 128 * out_ref.shape[0], 256):
        pick = jnp.where(dest_ref[...] == slot + first, 1.0, 0.0).astype(jnp.bfloat16)
        moved = nt(stacked, pick)
        moved = moved[:count] + (moved[count : 2 * count] + moved[2 * count :])
        for k in range(2):
            at = first // 128 + k
            value = moved[:, k * 128 : (k + 1) * 128]
            out_ref[at, 0:count, :] = value + old[0][at, 0:count, :] if old else value
            out_ref[at, count:, :] = tail


def place(groups, dest, parts, rows, old=()):
    whole = pl.BlockSpec(memory_space=pltpu.VMEM)
    return pl.pallas_call(
        functools.partial(place_kernel, len(parts)),
        grid=(1,),
        in_specs=[whole] * (1 + len(parts) + len(old)),
        out_specs=whole,
        out_shape=jax.ShapeDtypeStruct((groups, rows, 128), jnp.float32),
        compiler_params=pltpu.CompilerParams(vmem_limit_bytes=VMEM_LIMIT),
        cost_estimate=pl.CostEstimate(flops=10**9, bytes_accessed=4 * 1024 * 1024, transcendentals=0),
    )(dest[None, :], *parts, *old)


def finish_kernel(window, terms, base_ref, first_ref, got_ref, out_ref):
    rows = got_ref.shape[1] - 8
    both = [got_ref[k] + got_ref[NY + k] for k in range(NY)]
    values = jnp.transpose(jnp.concatenate([v[:rows] for v in both], axis=0))
    squares = jnp.concatenate(
        [w for v in both for w in (v[rows : rows + 1, :], v[rows + 1 : rows + 2, : rows - 128])],
        axis=1,
    )
    scale = lax.rsqrt(squares / terms + 1e-06)
    ids = base_ref[0] + lax.broadcasted_iota(jnp.int32, values.shape, 1)
    first = first_ref[...]
    inside = (ids >= first) & (ids < first + window)
    out_ref[...] = jnp.where(inside, values * scale, 0.0)


def finish(base, first, got, window, terms):
    whole = pl.BlockSpec(memory_space=pltpu.VMEM)
    return pl.pallas_call(
        functools.partial(finish_kernel, window, terms),
        in_specs=[pl.BlockSpec(memory_space=pltpu.SMEM), whole, whole],
        out_specs=whole,
        out_shape=jax.ShapeDtypeStruct((got.shape[2], NY * (got.shape[1] - 8)), jnp.float32),
        compiler_params=pltpu.CompilerParams(vmem_limit_bytes=VMEM_LIMIT),
    )(base, first[:, None], got)


def fence(*arrays):
    return lax.optimization_barrier(arrays)


def shards(train_grads, left_factor, right_factor, queries, owners, range_start):
    nmods = lax.axis_size("mod")
    nblk = lax.axis_size("blk")
    rows_dev = train_grads.shape[1]
    feat = train_grads.shape[2]
    side = left_factor.shape[1]
    qblock = queries.shape[1]
    half = qblock // 2
    window = rows_dev * nblk // 2
    grads = train_grads[0]
    m = lax.axis_index("mod")
    b = lax.axis_index("blk")
    z, h, c = b // 4, (b // 2) % 2, b % 2

    mats = queries[0].reshape(qblock, side, side)
    mats = jnp.einsum("rad,cd->rac", mats, right_factor[0], precision=lax.Precision.HIGH)
    mats = jnp.einsum("ba,rac->rbc", left_factor[0], mats, precision=lax.Precision.HIGH)
    own = mats.reshape(qblock, feat)

    own, grads = fence(own, grads)
    halves = []

    def ids(*named):
        for flip in range(2):
            for d, col, *ps in named:
                where = (z + d) % NZ * 4 + (h + col) % 2 * 2 + (c + flip) % 2
                halves.extend(where * 2 + p for p in (ps or (0, 1)))

    size = qblock
    a1m, a1p, e0 = up(own), down(own), far(own)
    a1m, a1p = fence(a1m, a1p)
    a2m, a2p, e1p = up(a1m), down(a1p), far(a1p)
    hi, lo, squares = split_grads(grads)
    a2m, a2p, e0, e1p, squares = fence(a2m, a2p, e0, e1p, squares)
    a3m, a3p, e1m = up(a2m), down(a2p), far(a1m)
    (near,) = pack([own, a1m, a1p, e0], [(k, 0, size) for k in range(4)])
    near_c = other(near)
    ids((0, 0), (-1, 0), (1, 0), (0, 1))
    part0 = scores_of((hi, lo), [(near, 0, 4 * size), (near_c, 0, 4 * size)], squares)
    a3m, a3p, e1m, part0 = fence(a3m, a3p, e1m, part0)
    for_up, for_down, for_far, three = pack(
        [a3m, a3p, e1m, e1p, a2m, a2p],
        [(0, 0, half), (2, 0, half)],
        [(1, half, half), (3, 0, half)],
        [(1, half, half), (0, half, half)],
        [(4, 0, size), (5, 0, size), (2, 0, size), (3, 0, size)],
    )
    up4, down4, far4 = up(for_up), down(for_down), far(for_far)
    three_c, part0 = fence(other(three), part0)
    got0 = over_y(part0)
    ids((-2, 0), (2, 0), (-1, 1), (1, 1))
    part1 = scores_of((hi, lo), [(three, 0, 4 * size), (three_c, 0, 4 * size)])
    up4, down4, far4, part1, got0 = fence(up4, down4, far4, part1, got0)
    for_up, for_down, for_far, four = pack(
        [up4, down4, far4, e1m, e1p, a3m, a3p],
        [(3, half, half), (0, half, half)],
        [(4, half, half), (1, half, half)],
        [(0, 0, half), (1, 0, half)],
        [(k, 0, size) for k in (5, 6, 0, 1, 2)],
    )
    up5, down5, far5 = up(for_up), down(for_down), far(for_far)
    four_c, part1 = fence(other(four), part1)
    got1 = over_y(part1)
    ids((-3, 0), (3, 0), (4, 0, 0), (-2, 1, 0), (4, 0, 1), (2, 1, 0))
    part2 = scores_of((hi, lo), [(four, 0, 4 * size), (four_c, 0, 4 * size)])
    up5, down5, far5, part2, got1 = fence(up5, down5, far5, part2, got1)
    (five,) = pack([up5, down5, far5], [(k, 0, size) for k in range(3)])
    five_c = other(five)
    got2 = over_y(part2)
    ids((3, 1, 1), (-3, 1, 1), (-2, 1, 1), (-3, 1, 0), (2, 1, 1), (3, 1, 0), (4, 1, 0), (4, 1, 1))
    part3 = scores_of(
        (hi, lo),
        [(four, 4 * size, size), (five, 0, 3 * size), (four_c, 4 * size, size), (five_c, 0, 3 * size)],
    )
    part3, got2 = fence(part3, got2)
    got3 = over_y(part3)

    source = jnp.stack(halves).astype(jnp.int32)
    blocks = jnp.arange(nblk, dtype=jnp.int32)
    target = jnp.sum(jnp.where((source // 2)[:, None] == blocks[None, :], owners[None, :], 0), axis=1)
    dest = ((target * 2 + source % 2) * half)[:, None] + jnp.arange(half, dtype=jnp.int32)[None, :]
    dest = dest.reshape(-1)
    early = got0.shape[2] + got1.shape[2] + got2.shape[2]
    groups, rows = dest.shape[0] // 128, got0.shape[1]
    placed = place(groups, dest[:early], [got0, got1, got2], rows)
    placed = place(groups, dest[early:], [got3], rows, [placed])
    got = lax.all_to_all(placed, "mod", 0, 0)
    out_block = m * (nblk // nmods) + jnp.arange(placed.shape[2], dtype=jnp.int32) // qblock
    first = jnp.sum(jnp.where(out_block[:, None] == blocks[None, :], range_start[None, :], 0), axis=1)
    base = jnp.reshape(b * rows_dev, (1,)).astype(jnp.int32)
    return finish(base, first, got, window, nmods * feat)


def solution(mesh):
    in_specs = (
        P("mod", "blk", None),
        P("mod", None, None),
        P("mod", None, None),
        P("mod", "blk", None),
        P(),
        P(),
    )
    out_specs = P("mod", "blk")
    return jax.shard_map(shards, mesh=mesh, in_specs=in_specs, out_specs=out_specs, check_vma=False)
```

```python
import functools

import jax
import jax.numpy as jnp
from jax import lax
from jax.experimental import pallas as pl
from jax.experimental.pallas import tpu as pltpu
from jax.sharding import PartitionSpec as P

NZ = 8
NY = 4
FEAT_STEP = 1024
VMEM_LIMIT = 16 * 1024 * 1024


def blk_pairs(move):
    return [
        (z * 4 + h * 2 + c, move(z, h, c))
        for z in range(NZ)
        for h in range(2)
        for c in range(2)
    ]


Z_UP = blk_pairs(lambda z, h, c: (z + 1) % NZ * 4 + h * 2 + c)
Z_DOWN = blk_pairs(lambda z, h, c: (z - 1) % NZ * 4 + h * 2 + c)
X_FAR = blk_pairs(lambda z, h, c: z * 4 + (1 - h) * 2 + c)
CORE = blk_pairs(lambda z, h, c: z * 4 + h * 2 + 1 - c)
Y_GROUPS = [[x * 4 + y for y in range(NY)] for x in range(2)]


def up(block):
    return lax.ppermute(block, "blk", Z_UP)


def down(block):
    return lax.ppermute(block, "blk", Z_DOWN)


def far(block):
    return lax.ppermute(block, "blk", X_FAR)


def other(block):
    return lax.ppermute(block, "blk", CORE)


def split(value):
    high = value.astype(jnp.bfloat16)
    low = (value - high.astype(jnp.float32)).astype(jnp.bfloat16)
    return high, low


def nt(a, b):
    return lax.dot_general(a, b, (((1,), (1,)), ((), ())), preferred_element_type=jnp.float32)


def split_kernel(g_ref, hi_ref, lo_ref, sq_ref):
    g = g_ref[...]
    high, low = split(g)
    for k in range(hi_ref.shape[0]):
        part = slice(k * FEAT_STEP, (k + 1) * FEAT_STEP)
        hi_ref[k], lo_ref[k] = high[:, part], low[:, part]
    sq_ref[...] = jnp.broadcast_to(jnp.sum(g * g, axis=1, keepdims=True), sq_ref.shape)


def split_grads(grads):
    rows, feat = grads.shape
    steps = feat // FEAT_STEP
    piece = pl.BlockSpec((steps, 64, FEAT_STEP), lambda i: (0, i, 0))
    return pl.pallas_call(
        split_kernel,
        grid=(rows // 64,),
        in_specs=[pl.BlockSpec((64, feat), lambda i: (i, 0))],
        out_specs=[piece, piece, pl.BlockSpec((64, 128), lambda i: (i, 0))],
        out_shape=[
            pltpu.HBM((steps, rows, FEAT_STEP), jnp.bfloat16),
            pltpu.HBM((steps, rows, FEAT_STEP), jnp.bfloat16),
            jax.ShapeDtypeStruct((rows, 128), jnp.float32),
        ],
        compiler_params=pltpu.CompilerParams(vmem_limit_bytes=VMEM_LIMIT),
    )(pltpu.with_memory_space_constraint(grads, pltpu.HBM))


def score_kernel(spans, squares, hi_ref, lo_ref, *refs):
    sq_ref = None
    if squares:
        sq_ref, *refs = refs
    pieces = refs[: len(spans)]
    out_ref, acc = refs[len(spans) :]
    step = pl.program_id(0)
    rows = acc.shape[0]
    q = jnp.concatenate([p[a:b, :] for p, (a, b) in zip(pieces, spans)], axis=0)
    qhi, qlo = split(q)
    ghi, glo = hi_ref[0], lo_ref[0]
    value = nt(ghi, qhi) + (nt(ghi, qlo) + nt(glo, qhi))

    @pl.when(step == 0)
    def _():
        acc[...] = value

    @pl.when(step > 0)
    def _():
        acc[...] += value

    @pl.when(step == pl.num_programs(0) - 1)
    def _():
        emit(sq_ref, acc, out_ref)


def emit(sq_ref, acc, out_ref):
    count = acc.shape[0] // NY
    for k in range(NY):
        here = slice(k * count, (k + 1) * count)
        out_ref[k, 0:count, :] = acc[here, :]
        if sq_ref is not None:
            out_ref[k, count:, :] = jnp.zeros((8, out_ref.shape[2]), jnp.float32)
            out_ref[k, count:, 0:count] = jnp.transpose(sq_ref[here, 0:8])


def scores_of(grads, pieces, squares=None):
    hi, lo = (pltpu.with_memory_space_constraint(g, pltpu.HBM) for g in grads)
    steps, rows, wide = hi.shape
    spans = [(first, first + count) for _, first, count in pieces]
    width = sum(count for _, _, count in pieces)
    slice_rows = rows // NY + (0 if squares is None else 8)
    whole = pl.BlockSpec(memory_space=pltpu.VMEM)
    extra = [] if squares is None else [squares]
    flops = 6 * rows * width * steps * wide
    return pl.pallas_call(
        functools.partial(score_kernel, spans, squares is not None),
        grid=(steps,),
        in_specs=[pl.BlockSpec((1, rows, wide), lambda i: (i, 0, 0))] * 2
        + [whole] * len(extra)
        + [pl.BlockSpec((p[0].shape[0], wide), lambda i: (0, i)) for p in pieces],
        out_specs=whole,
        out_shape=jax.ShapeDtypeStruct((NY, slice_rows, width), jnp.float32),
        scratch_shapes=[pltpu.VMEM((rows, width), jnp.float32)],
        compiler_params=pltpu.CompilerParams(vmem_limit_bytes=VMEM_LIMIT),
        cost_estimate=pl.CostEstimate(flops=flops, bytes_accessed=4 * 1024 * 1024, transcendentals=0),
    )(hi, lo, *extra, *[p[0] for p in pieces])


def over_y(slices):
    return lax.all_to_all(slices, "mod", 0, 0, axis_index_groups=Y_GROUPS)


def pack_kernel(plans, *refs):
    blocks, outs = refs[: -len(plans)], refs[-len(plans) :]
    for out, plan in zip(outs, plans):
        at = 0
        for which, first, count in plan:
            out[at : at + count, :] = blocks[which][first : first + count, :]
            at += count


def pack(blocks, *plans):
    whole = pl.BlockSpec(memory_space=pltpu.VMEM)
    return pl.pallas_call(
        functools.partial(pack_kernel, plans),
        in_specs=[whole] * len(blocks),
        out_specs=[whole] * len(plans),
        out_shape=[
            jax.ShapeDtypeStruct((sum(p[2] for p in plan), blocks[0].shape[1]), jnp.float32)
            for plan in plans
        ],
        compiler_params=pltpu.CompilerParams(vmem_limit_bytes=VMEM_LIMIT),
    )(*blocks)


def place_kernel(nparts, dest_ref, *refs):
    parts, (*old, out_ref) = refs[:nparts], refs[nparts:]
    sums = [p[0] + p[1] + (p[2] + p[3]) for p in parts]
    count = parts[-1].shape[1]
    total = jnp.concatenate([v[:count] for v in sums], axis=1)
    high = total.astype(jnp.bfloat16)
    rest = total - high.astype(jnp.float32)
    mid = rest.astype(jnp.bfloat16)
    low = (rest - mid.astype(jnp.float32)).astype(jnp.bfloat16)
    stacked = jnp.concatenate([high, mid, low], axis=0)
    if old:
        tail = old[0][0, count:, :]
    else:
        squares = sums[0][count:, :]
        row = lax.broadcasted_iota(jnp.int32, (8, 128), 0)
        tail = jnp.where(row == 0, squares[:, 0:128], squares[:, 128:256])
    slot = lax.broadcasted_iota(jnp.int32, (256, total.shape[1]), 0)
    for first in range(0, 128 * out_ref.shape[0], 256):
        pick = jnp.where(dest_ref[...] == slot + first, 1.0, 0.0).astype(jnp.bfloat16)
        moved = nt(stacked, pick)
        moved = moved[:count] + (moved[count : 2 * count] + moved[2 * count :])
        for k in range(2):
            at = first // 128 + k
            value = moved[:, k * 128 : (k + 1) * 128]
            out_ref[at, 0:count, :] = value + old[0][at, 0:count, :] if old else value
            out_ref[at, count:, :] = tail


def place(groups, dest, parts, rows, old=()):
    whole = pl.BlockSpec(memory_space=pltpu.VMEM)
    return pl.pallas_call(
        functools.partial(place_kernel, len(parts)),
        grid=(1,),
        in_specs=[whole] * (1 + len(parts) + len(old)),
        out_specs=whole,
        out_shape=jax.ShapeDtypeStruct((groups, rows, 128), jnp.float32),
        compiler_params=pltpu.CompilerParams(vmem_limit_bytes=VMEM_LIMIT),
        cost_estimate=pl.CostEstimate(flops=10**9, bytes_accessed=4 * 1024 * 1024, transcendentals=0),
    )(dest[None, :], *parts, *old)


def finish_kernel(window, terms, base_ref, first_ref, got_ref, out_ref):
    rows = got_ref.shape[1] - 8
    both = [got_ref[k] + got_ref[NY + k] for k in range(NY)]
    values = jnp.transpose(jnp.concatenate([v[:rows] for v in both], axis=0))
    squares = jnp.concatenate(
        [w for v in both for w in (v[rows : rows + 1, :], v[rows + 1 : rows + 2, : rows - 128])],
        axis=1,
    )
    scale = lax.rsqrt(squares / terms + 1e-06)
    ids = base_ref[0] + lax.broadcasted_iota(jnp.int32, values.shape, 1)
    first = first_ref[...]
    inside = (ids >= first) & (ids < first + window)
    out_ref[...] = jnp.where(inside, values * scale, 0.0)


def finish(base, first, got, window, terms):
    whole = pl.BlockSpec(memory_space=pltpu.VMEM)
    return pl.pallas_call(
        functools.partial(finish_kernel, window, terms),
        in_specs=[pl.BlockSpec(memory_space=pltpu.SMEM), whole, whole],
        out_specs=whole,
        out_shape=jax.ShapeDtypeStruct((got.shape[2], NY * (got.shape[1] - 8)), jnp.float32),
        compiler_params=pltpu.CompilerParams(vmem_limit_bytes=VMEM_LIMIT),
    )(base, first[:, None], got)


def fence(*arrays):
    return lax.optimization_barrier(arrays)


def shards(train_grads, left_factor, right_factor, queries, owners, range_start):
    nmods = lax.axis_size("mod")
    nblk = lax.axis_size("blk")
    rows_dev = train_grads.shape[1]
    feat = train_grads.shape[2]
    side = left_factor.shape[1]
    qblock = queries.shape[1]
    half = qblock // 2
    window = rows_dev * nblk // 2
    grads = train_grads[0]
    m = lax.axis_index("mod")
    b = lax.axis_index("blk")
    z, h, c = b // 4, (b // 2) % 2, b % 2

    mats = queries[0].reshape(qblock, side, side)
    mats = jnp.einsum("rad,cd->rac", mats, right_factor[0], precision=lax.Precision.HIGHEST)
    mats = jnp.einsum("ba,rac->rbc", left_factor[0], mats, precision=lax.Precision.HIGHEST)
    own = mats.reshape(qblock, feat)

    own, grads = fence(own, grads)
    halves = []

    def ids(*named):
        for flip in range(2):
            for d, col, *ps in named:
                where = (z + d) % NZ * 4 + (h + col) % 2 * 2 + (c + flip) % 2
                halves.extend(where * 2 + p for p in (ps or (0, 1)))

    size = qblock
    a1m, a1p, e0 = up(own), down(own), far(own)
    a1m, a1p = fence(a1m, a1p)
    a2m, a2p, e1p = up(a1m), down(a1p), far(a1p)
    hi, lo, squares = split_grads(grads)
    a2m, a2p, e0, e1p, squares = fence(a2m, a2p, e0, e1p, squares)
    a3m, a3p, e1m = up(a2m), down(a2p), far(a1m)
    (near,) = pack([own, a1m, a1p, e0], [(k, 0, size) for k in range(4)])
    near_c = other(near)
    ids((0, 0), (-1, 0), (1, 0), (0, 1))
    part0 = scores_of((hi, lo), [(near, 0, 4 * size), (near_c, 0, 4 * size)], squares)
    a3m, a3p, e1m, part0 = fence(a3m, a3p, e1m, part0)
    for_up, for_down, for_far, three = pack(
        [a3m, a3p, e1m, e1p, a2m, a2p],
        [(0, 0, half), (2, 0, half)],
        [(1, half, half), (3, 0, half)],
        [(1, half, half), (0, half, half)],
        [(4, 0, size), (5, 0, size), (2, 0, size), (3, 0, size)],
    )
    up4, down4, far4 = up(for_up), down(for_down), far(for_far)
    three_c = other(three)
    part0 = fence(three_c[:8, :128], part0)[1]
    got0 = over_y(part0)
    ids((-2, 0), (2, 0), (-1, 1), (1, 1))
    part1 = scores_of((hi, lo), [(three, 0, 4 * size), (three_c, 0, 4 * size)])
    up4, down4, far4, part1, got0 = fence(up4, down4, far4, part1, got0)
    for_up, for_down, for_far, four = pack(
        [up4, down4, far4, e1m, e1p, a3m, a3p],
        [(3, half, half), (0, half, half)],
        [(4, half, half), (1, half, half)],
        [(0, 0, half), (1, 0, half)],
        [(k, 0, size) for k in (5, 6, 0, 1, 2)],
    )
    up5, down5, far5 = up(for_up), down(for_down), far(for_far)
    four_c = other(four)
    part1 = fence(four_c[:8, :128], part1)[1]
    got1 = over_y(part1)
    ids((-3, 0), (3, 0), (4, 0, 0), (-2, 1, 0), (4, 0, 1), (2, 1, 0))
    part2 = scores_of((hi, lo), [(four, 0, 4 * size), (four_c, 0, 4 * size)])
    up5, down5, far5, part2, got1 = fence(up5, down5, far5, part2, got1)
    (five,) = pack([up5, down5, far5], [(k, 0, size) for k in range(3)])
    five_c = other(five)
    got2 = over_y(part2)
    ids((3, 1, 1), (-3, 1, 1), (-2, 1, 1), (-3, 1, 0), (2, 1, 1), (3, 1, 0), (4, 1, 0), (4, 1, 1))
    part3 = scores_of(
        (hi, lo),
        [(four, 4 * size, size), (five, 0, 3 * size), (four_c, 4 * size, size), (five_c, 0, 3 * size)],
    )
    part3, got2 = fence(part3, got2)
    got3 = over_y(part3)

    source = jnp.stack(halves).astype(jnp.int32)
    blocks = jnp.arange(nblk, dtype=jnp.int32)
    target = jnp.sum(jnp.where((source // 2)[:, None] == blocks[None, :], owners[None, :], 0), axis=1)
    dest = ((target * 2 + source % 2) * half)[:, None] + jnp.arange(half, dtype=jnp.int32)[None, :]
    dest = dest.reshape(-1)
    early = got0.shape[2] + got1.shape[2] + got2.shape[2]
    groups, rows = dest.shape[0] // 128, got0.shape[1]
    placed = place(groups, dest[:early], [got0, got1, got2], rows)
    placed = place(groups, dest[early:], [got3], rows, [placed])
    got = lax.all_to_all(placed, "mod", 0, 0)
    out_block = m * (nblk // nmods) + jnp.arange(placed.shape[2], dtype=jnp.int32) // qblock
    first = jnp.sum(jnp.where(out_block[:, None] == blocks[None, :], range_start[None, :], 0), axis=1)
    base = jnp.reshape(b * rows_dev, (1,)).astype(jnp.int32)
    return finish(base, first, got, window, nmods * feat)


def solution(mesh):
    in_specs = (
        P("mod", "blk", None),
        P("mod", None, None),
        P("mod", None, None),
        P("mod", "blk", None),
        P(),
        P(),
    )
    out_specs = P("mod", "blk")
    return jax.shard_map(shards, mesh=mesh, in_specs=in_specs, out_specs=out_specs, check_vma=False)
```
